32 devices in a mesh: groups: 2 (over x), seq: 16 (over z, y, core).
Axes of the slice: x: 2, y: 2, z: 4, core: 2. Of those that a mesh axis runs over, the one named last changes fastest.
Arguments:
- window_queries: bfloat16 [4096, 2048], P(('groups', 'seq')), parts along dimension 0, may hold values from -300 to 300
- window_kv: bfloat16 [4096, 512], P(('groups', 'seq')), parts along dimension 0, may hold values from -6 to 6
- stream: bfloat16 [4096, 2880], P(('groups', 'seq')), parts along dimension 0, may hold values from -6 to 6
- moe_gain: float32 [2880], replicated, may hold values from 0.25 to 1.75
- routes: int32 [4096, 4], P(('groups', 'seq')), parts along dimension 0, may hold values from 0 to 15, as said below
- route_gates: float32 [4096, 4], P(('groups', 'seq')), parts along dimension 0, may hold values from 0.1 to 0.6
- gate_proj: bfloat16 [2880, 23040], P(None, 'seq'), may hold values from -0.109375 to 0.109375
- up_proj: bfloat16 [2880, 23040], P(None, 'seq'), may hold values from -0.109375 to 0.109375
- down_proj: bfloat16 [23040, 2880], P('seq'), may hold values from -0.15625 to 0.15625
- attn_gain: float32 [2880], replicated, may hold values from 0.25 to 1.75
- kv_proj: bfloat16 [2880, 512], replicated, may hold values from -0.109375 to 0.109375
- tract_queries: bfloat16 [4096, 2048], P(('groups', 'seq')), parts along dimension 0, may hold values from -300 to 300
Outputs:
- attn_window: bfloat16 [4096, 2048], P(('groups', 'seq')), parts along dimension 0
- stream_next: bfloat16 [4096, 2880], P(('groups', 'seq')), parts along dimension 0
- attn_tract: bfloat16 [4096, 2048], P(('groups', 'seq')), parts along dimension 0
The draws below stay inside these ranges and needn't reach their ends.
There are 2 independent parts, one for each index of `groups`. The reference program is written for one: setup_inputs(seed, part) draws one part's arguments, and reference() takes and returns one part's arrays. A program takes and returns all parts, laid end to end along the dimension named above; an argument that names none is the same for every part. Nothing has to cross between parts.
Inputs may be any that keep to these rules, and one draw needn't show every extreme that they name: `routes`: in each device's block of 128 tokens every expert is named exactly 32 times; a token names 4 different experts.
All inputs are finite; a program needn't handle non-finite values.
Results may differ from the reference program's by a relative error of at most 0.025.
The reference program's roundings to bfloat16 on the way (of `attend`, `moe_input`, `hidden`, `block_out`, `attn_input` and `tract_kv`) count: a program that leaves them out, or rounds other values in their place, can miss the bound.
Values may be sent and summed in bfloat16 or wider, within the bound.
A program may use at most 128 MiB of HBM per device.

```python
import jax
import jax.numpy as jnp
from jax import lax

D = 2880
HEADS = 32
KV_HEADS = 4
HEAD_DIM = 64
EXPERTS = 16
FF = 1440
TOP = 4
WINDOW = 128
STRETCH = 1024
TOK_DEV = 128
TOKENS = 2048
CAP = 32
SPLIT = 1
PIECE = 1440
N_SEQ = 16


def query_draw(key):
    values = jnp.clip(jax.random.normal(key, (TOKENS, HEADS * HEAD_DIM), jnp.float32), -6.0, 6.0)
    return values.astype(jnp.bfloat16)


def draw_window_queries(key, part):
    return query_draw(jax.random.fold_in(key, 11))


def draw_tract_queries(key, part):
    return query_draw(jax.random.fold_in(key, 23))


def route_block(key):
    group_size = EXPERTS // TOP
    labels = jax.random.permutation(jax.random.fold_in(key, 1), EXPERTS).astype(jnp.int32)
    row_index = jnp.arange(TOK_DEV, dtype=jnp.int32)
    col_index = jnp.arange(TOP, dtype=jnp.int32)
    base_table = labels[col_index[None, :] * group_size + row_index[:, None] // CAP]

    def column_order(index):
        return jax.random.permutation(jax.random.fold_in(key, 100 + index), TOK_DEV).astype(jnp.int32)
    orders = jax.vmap(column_order)(col_index)
    route_table = base_table[jnp.transpose(orders), col_index[None, :]]
    half_rows = TOK_DEV // 2
    upper_rows = route_table[:half_rows]
    lower_rows = route_table[half_rows:]
    coin_flip = jax.random.randint(jax.random.fold_in(key, 2), (half_rows,), 0, 2) == 1
    swap_ok = coin_flip & (upper_rows[:, 1] != lower_rows[:, 1]) & (upper_rows[:, 0] != lower_rows[:, 0])
    upper_first = jnp.where(swap_ok, lower_rows[:, 1], upper_rows[:, 0])
    lower_second = jnp.where(swap_ok, upper_rows[:, 0], lower_rows[:, 1])
    upper_rows = upper_rows.at[:, 0].set(upper_first)
    lower_rows = lower_rows.at[:, 1].set(lower_second)
    route_table = jnp.concatenate([upper_rows, lower_rows], 0)
    turn_by = jax.random.randint(jax.random.fold_in(key, 3), (TOK_DEV, 1), 0, TOP)
    route_table = jnp.take_along_axis(route_table, (col_index[None, :] + turn_by) % TOP, axis=1)
    return route_table.astype(jnp.int32)


def draw_routes(key, part):
    block_count = TOKENS // TOK_DEV
    base_key = jax.random.fold_in(key, 31)
    block_keys = jax.vmap(lambda index: jax.random.fold_in(base_key, index))(jnp.arange(block_count, dtype=jnp.int32))
    tables = jax.vmap(route_block)(block_keys)
    return tables.reshape(TOKENS, TOP).astype(jnp.int32)


def steps_of(key, extent, split, smallest, largest):
    factor_of, own = 1.0, jax.random.fold_in(key, 6)
    for position, shards_of in split:
        heights = jnp.exp(jax.random.uniform(jax.random.fold_in(own, position), (shards_of,), jnp.float32, smallest / len(split), largest / len(split)))
        factor_of = factor_of * jnp.repeat(heights, extent[position] // shards_of).reshape([-1 if axis == position else 1 for axis in range(len(extent))])
    return factor_of


def scatter_about(own_key, shape, spread, most, split=(), kind=jnp.bfloat16):
    loudness = steps_of(own_key, shape, split, -0.22, 0.18) if split else 1.0
    array = jax.random.normal(own_key, shape, jnp.float32) * spread * loudness
    return jnp.minimum(jnp.maximum(array, -most), most).astype(kind)


def setup_inputs(seed: int = 0, part: int = 0) -> dict:
    arg_keys = jax.random.split(jax.random.key(seed), 13)
    part_keys = jax.random.split(jax.random.fold_in(arg_keys[12], part), 13)
    return {
        "window_queries": draw_window_queries(jax.random.fold_in(jax.random.fold_in(arg_keys[12], part), 71), part),
        "window_kv": scatter_about(part_keys[1], (TOKENS, 2 * KV_HEADS * HEAD_DIM), 1.0, 6.0, ((0, 16),)),
        "stream": scatter_about(part_keys[2], (TOKENS, D), 1.0, 6.0, ((0, 16),)),
        "moe_gain": jnp.clip(1.0 + 0.15 * jax.random.normal(arg_keys[3], (D,), jnp.float32), 0.25, 1.75),
        "routes": draw_routes(jax.random.fold_in(jax.random.fold_in(arg_keys[12], part), 71), part),
        "route_gates": jnp.clip(0.1 + 0.5 * jax.random.uniform(part_keys[5], (TOKENS, TOP), jnp.float32) ** steps_of(part_keys[5], (TOKENS, TOP), ((0, 16),), -0.2, 0.2), 0.1, 0.6),
        "gate_proj": scatter_about(arg_keys[6], (D, EXPERTS * FF), D ** -0.5, 0.109375, ((1, 16),)),
        "up_proj": scatter_about(arg_keys[7], (D, EXPERTS * FF), D ** -0.5, 0.109375, ((1, 16),)),
        "down_proj": scatter_about(arg_keys[8], (EXPERTS * FF, D), FF ** -0.5, 0.15625, ((0, 16),)),
        "attn_gain": jnp.clip(1.0 + 0.15 * jax.random.normal(arg_keys[9], (D,), jnp.float32), 0.25, 1.75),
        "kv_proj": scatter_about(arg_keys[10], (D, 2 * KV_HEADS * HEAD_DIM), D ** -0.5, 0.109375),
        "tract_queries": draw_tract_queries(jax.random.fold_in(jax.random.fold_in(arg_keys[12], part), 71), part),
    }


def normed(values, gain):
    widened = values.astype(jnp.float32)
    second = lax.optimization_barrier(jnp.mean(widened * widened, axis=-1, keepdims=True))
    return (widened * lax.rsqrt(second + 1e-05) * gain).astype(jnp.bfloat16)

def attend(queries, keys, values, allowed):
    query_rows = queries.shape[0]
    key_rows = keys.shape[0]
    group_size = HEADS // KV_HEADS
    query_heads = queries.astype(jnp.float32).reshape(query_rows, KV_HEADS, group_size, HEAD_DIM)
    key_heads = keys.astype(jnp.float32).reshape(key_rows, KV_HEADS, HEAD_DIM)
    value_heads = values.astype(jnp.float32).reshape(key_rows, KV_HEADS, HEAD_DIM)
    scores = jnp.einsum('qkgd,skd->kgqs', query_heads, key_heads) * 0.125
    scores = jnp.where(allowed, scores, -1e+30)
    peak = lax.optimization_barrier(jnp.max(scores, axis=-1, keepdims=True))
    weights = jnp.exp(scores - peak)
    totals = lax.optimization_barrier(jnp.sum(weights, axis=-1))
    rounded = lax.optimization_barrier(weights.astype(jnp.bfloat16)).astype(jnp.float32)
    mixed = jnp.einsum('kgqs,skd->qkgd', rounded, value_heads)
    mixed = mixed / jnp.transpose(totals, (2, 0, 1))[..., None]
    return mixed.reshape(query_rows, HEADS * HEAD_DIM).astype(jnp.bfloat16)

def reference(window_queries, window_kv, stream, moe_gain, routes, route_gates, gate_proj, up_proj, down_proj, attn_gain, kv_proj, tract_queries):
    half_cols = KV_HEADS * HEAD_DIM
    query_block = min(512, TOKENS)
    padded = jnp.concatenate([jnp.zeros((WINDOW, 2 * half_cols), jnp.bfloat16), window_kv], 0)

    def window_block(block_index):
        offset = block_index * query_block
        queries = lax.dynamic_slice_in_dim(window_queries, offset, query_block, 0)
        nearby = lax.dynamic_slice_in_dim(padded, offset, query_block + WINDOW, 0)
        query_pos = offset + jnp.arange(query_block, dtype=jnp.int32)
        key_pos = offset - WINDOW + jnp.arange(query_block + WINDOW, dtype=jnp.int32)
        distance = query_pos[:, None] - key_pos[None, :]
        allowed = (distance >= 0) & (distance < WINDOW) & (key_pos[None, :] >= 0)
        return attend(queries, nearby[:, :half_cols], nearby[:, half_cols:], allowed)
    attn_window = lax.map(window_block, jnp.arange(TOKENS // query_block, dtype=jnp.int32)).reshape(TOKENS, HEADS * HEAD_DIM)
    moe_input = normed(stream, moe_gain)
    flat_routes = routes.reshape(N_SEQ, TOK_DEV * TOP)
    onehot = (flat_routes[:, :, None] == jnp.arange(EXPERTS, dtype=jnp.int32)[None, None, :]).astype(jnp.int32)
    slot_rank = lax.optimization_barrier(jnp.sum(onehot * (jnp.cumsum(onehot, axis=1) - 1), axis=2))
    device_rows = jnp.arange(N_SEQ, dtype=jnp.int32)[:, None]
    token_ids = device_rows * TOK_DEV + jnp.arange(TOK_DEV * TOP, dtype=jnp.int32)[None, :] // TOP
    slot_index = flat_routes * CAP + slot_rank
    slot_table = jnp.zeros((N_SEQ, EXPERTS * CAP), jnp.int32).at[device_rows, slot_index].set(token_ids)
    gathered = moe_input[slot_table].reshape(N_SEQ, EXPERTS, CAP, D)

    def expert_out(expert):
        expert_rows = lax.dynamic_index_in_dim(gathered, expert, 1, keepdims=False).reshape(N_SEQ * CAP, D)
        summed = jnp.zeros((N_SEQ * CAP, D), jnp.float32)
        for part_index in range(SPLIT):
            first_col = expert * FF + part_index * PIECE
            gate_cols = lax.dynamic_slice_in_dim(gate_proj, first_col, PIECE, 1)
            up_cols = lax.dynamic_slice_in_dim(up_proj, first_col, PIECE, 1)
            down_rows = lax.dynamic_slice_in_dim(down_proj, first_col, PIECE, 0)
            gate_vals = jnp.dot(expert_rows, gate_cols, preferred_element_type=jnp.float32)
            up_vals = jnp.dot(expert_rows, up_cols, preferred_element_type=jnp.float32)
            hidden = (jax.nn.silu(gate_vals) * up_vals).astype(jnp.bfloat16)
            block_out = jnp.dot(hidden, down_rows, preferred_element_type=jnp.float32).astype(jnp.bfloat16)
            summed = summed + block_out.astype(jnp.float32)
        return summed.reshape(N_SEQ, CAP, D)
    outputs = lax.map(expert_out, jnp.arange(EXPERTS, dtype=jnp.int32))
    flat_out = outputs.reshape(EXPERTS * N_SEQ * CAP, D)
    picked_index = ((flat_routes * N_SEQ + device_rows) * CAP + slot_rank).reshape(-1)
    picked = flat_out[picked_index].reshape(TOKENS, TOP, D)
    stream_next = (stream.astype(jnp.float32) + lax.optimization_barrier(jnp.sum(picked * route_gates[:, :, None], axis=1))).astype(jnp.bfloat16)
    attn_input = normed(stream_next, attn_gain)
    tract_kv = jnp.dot(attn_input, kv_proj, preferred_element_type=jnp.float32).astype(jnp.bfloat16)
    lead = STRETCH // 2
    padded_kv = jnp.concatenate([jnp.zeros((lead, 2 * half_cols), jnp.bfloat16), tract_kv], 0)

    def stretch_block(block_index):
        offset = block_index * STRETCH
        queries = lax.dynamic_slice_in_dim(tract_queries, offset, STRETCH, 0)
        context = lax.dynamic_slice_in_dim(padded_kv, offset, STRETCH + lead, 0)
        query_pos = offset + jnp.arange(STRETCH, dtype=jnp.int32)
        key_pos = offset - lead + jnp.arange(STRETCH + lead, dtype=jnp.int32)
        allowed = (key_pos[None, :] <= query_pos[:, None]) & (key_pos[None, :] >= 0) & ((key_pos[None, :] + lead) // STRETCH == (query_pos[:, None] + lead) // STRETCH)
        return attend(queries, context[:, :half_cols], context[:, half_cols:], allowed)
    attn_tract = lax.map(stretch_block, jnp.arange(TOKENS // STRETCH, dtype=jnp.int32)).reshape(TOKENS, HEADS * HEAD_DIM)
    return (attn_window, stream_next, attn_tract)
```

```python
import functools

import jax
import jax.numpy as jnp
from jax import lax
from jax.experimental import pallas as pl
from jax.experimental.pallas import tpu as pltpu
from jax.sharding import PartitionSpec as P

HEADS = 32
KV_HEADS = 4
HEAD_DIM = 64
EXPERTS = 16
TOP = 4
WINDOW = 128
STRETCH = 1024
LOG2E = 1.4426950408889634
TILE = 512
BUNCH = 4


def tiles(width, tile=TILE):
    return [(at, min(tile, width - at)) for at in range(0, width, tile)]


def normed(values, gain):
    widened = values.astype(jnp.float32)
    second = jnp.mean(widened * widened, axis=-1, keepdims=True)
    return (widened * lax.rsqrt(second + 1e-05) * gain).astype(jnp.bfloat16)


def attend_into(q_ref, read, keys, bias_ref, kx, vx, out_ref):
    half_cols = KV_HEADS * HEAD_DIM
    lane = lax.broadcasted_iota(jnp.int32, (keys, 128), 1) // HEAD_DIM
    pairs = HEADS // KV_HEADS // 2

    @pl.loop(0, KV_HEADS)
    def _(kv):
        side = kv % 2
        for base, ext in ((0, kx), (half_cols, vx)):
            col = pl.multiple_of(base + (kv // 2) * 128, 128)
            both = read(col).astype(jnp.float32)
            same = jnp.where(lane == side, both, 0.0)
            ext[side, 0:keys, :] = same.astype(jnp.bfloat16)
            ext[1 - side, 0:keys, :] = pltpu.roll(same, HEAD_DIM, 1).astype(jnp.bfloat16)

        @pl.loop(0, pairs)
        def _(pair):
            cols = pl.ds(pl.multiple_of((kv * pairs + pair) * 128, 128), 128)
            query = q_ref[:, cols]
            total_out = None
            for parity in range(2):
                scores = lax.dot_general(
                    query, kx[parity, 0:keys, :], (((1,), (1,)), ((), ())),
                    preferred_element_type=jnp.float32,
                ) + bias_ref[...]
                peak = jnp.max(scores, axis=-1, keepdims=True)
                weights = jnp.exp2((scores - peak) * (0.125 * LOG2E))
                totals = jnp.sum(weights, axis=-1, keepdims=True)
                mixed = jnp.dot(
                    weights.astype(jnp.bfloat16), vx[parity, 0:keys, :],
                    preferred_element_type=jnp.float32,
                ) / totals
                total_out = mixed if total_out is None else total_out + mixed
            out_ref[:, cols] = total_out.astype(jnp.bfloat16)


def kernel(
    n, split, back,
    stream, moe_gain, routes_t, gates_t, attn_gain, window_kv,
    window_q_hbm, tract_q_hbm, gate_hbm, up_hbm, down_hbm, proj_hbm,
    window_out, next_out, tract_out,
    wq, tq, wg, wu, wd, wp, send, recv, hid, outs, ret, combine, rim, tkv, ctx, bias_w, bias_t, kx, vx,
    load_sem, send_sem, recv_sem, back_send_sem, back_recv_sem, rim_sem, tract_send, tract_recv,
):
    me = lax.axis_index("seq")
    rows, width = stream.shape
    cap = send.shape[1]
    ff = wg.shape[1]
    loads = [
        pltpu.make_async_copy(src, dst, load_sem.at[i])
        for i, (src, dst) in enumerate(
            ((window_q_hbm, wq), (gate_hbm, wg), (up_hbm, wu), (down_hbm, wd), (proj_hbm, wp), (tract_q_hbm, tq))
        )
    ]

    rim[...] = jnp.zeros_like(rim)
    ctx[...] = jnp.zeros_like(ctx)

    barrier = pltpu.get_barrier_semaphore()

    @pl.loop(1, n)
    def _(d):
        pl.semaphore_signal(barrier, inc=1, device_id={"seq": (me + d) % n}, device_id_type=pl.DeviceIdType.MESH)

    for load in loads:
        load.start()

    expert_id = lax.broadcasted_iota(jnp.int32, (EXPERTS, rows), 0)
    named = jnp.zeros((EXPERTS, rows), jnp.float32)
    gate_of = jnp.zeros((EXPERTS, rows), jnp.float32)
    for k in range(TOP):
        hit = routes_t[k : k + 1, :] == expert_id
        named = named + jnp.where(hit, 1.0, 0.0)
        gate_of = gate_of + jnp.where(hit, gates_t[k : k + 1, :], 0.0)
    earlier = lax.broadcasted_iota(jnp.int32, (rows, rows), 0) < lax.broadcasted_iota(jnp.int32, (rows, rows), 1)
    rank = jnp.dot(
        named.astype(jnp.bfloat16), jnp.where(earlier, 1.0, 0.0).astype(jnp.bfloat16),
        preferred_element_type=jnp.float32,
    )
    rank = jnp.where(named > 0.5, rank, -1.0)
    slot = lax.broadcasted_iota(jnp.int32, (EXPERTS, cap, rows), 1).astype(jnp.float32)
    pick = jnp.where(rank[:, None, :] == slot, 1.0, 0.0)
    moe_input = normed(stream[...], moe_gain[...])
    pick_flat = pick.reshape(EXPERTS * cap, rows).astype(jnp.bfloat16)
    for at, size in tiles(width):
        chosen = jnp.dot(pick_flat, moe_input[:, at : at + size], preferred_element_type=jnp.float32)
        send[:, :, at : at + size] = chosen.astype(jnp.bfloat16).reshape(EXPERTS, cap, size)

    pl.semaphore_wait(barrier, n - 1)

    def dispatch(dst, src):
        return pltpu.make_async_remote_copy(
            src_ref=send.at[dst // split], dst_ref=recv.at[src], send_sem=send_sem.at[dst], recv_sem=recv_sem.at[src],
            device_id={"seq": dst}, device_id_type=pl.DeviceIdType.MESH,
        )

    def give_back(dst, src):
        return pltpu.make_async_remote_copy(
            src_ref=outs.at[dst], dst_ref=ret.at[src], send_sem=back_send_sem.at[dst], recv_sem=back_recv_sem.at[src],
            device_id={"seq": dst}, device_id_type=pl.DeviceIdType.MESH,
        )

    def rim_copy(dst):
        return pltpu.make_async_remote_copy(
            src_ref=window_kv, dst_ref=rim, send_sem=rim_sem.at[0], recv_sem=rim_sem.at[1],
            device_id={"seq": dst}, device_id_type=pl.DeviceIdType.MESH,
        )

    @pl.when(me < n - 1)
    def _():
        rim_copy((me + 1) % n).start()

    @pl.loop(1, n)
    def _(d):
        dispatch((me + d) % n, me).start()

    recv[me] = send[me // split]

    gated = (pick * gate_of[:, None, :])[:, None]
    gated = jnp.broadcast_to(gated, (EXPERTS, split, cap, rows)).reshape(n * cap, rows)
    rest = gated.T
    for i in range(3):
        term = rest.astype(jnp.bfloat16)
        combine[i] = term
        rest = rest - term.astype(jnp.float32)

    row_w = lax.broadcasted_iota(jnp.int32, (rows, rows + WINDOW), 0)
    col_w = lax.broadcasted_iota(jnp.int32, (rows, rows + WINDOW), 1)
    distance = row_w - (col_w - WINDOW)
    seen = (distance >= 0) & (distance < WINDOW) & (me * rows + col_w - WINDOW >= 0)
    bias_w[...] = jnp.where(seen, 0.0, -1e30)
    first = me * rows
    row_t = lax.broadcasted_iota(jnp.int32, bias_t.shape, 0) + first
    col_t = lax.broadcasted_iota(jnp.int32, bias_t.shape, 1) + (first - back * rows)
    lead = STRETCH // 2
    tract = (first + lead) // STRETCH
    start = tract * STRETCH - lead
    seen = (col_t <= row_t) & (col_t >= 0) & (col_t >= start)
    bias_t[...] = jnp.where(seen, 0.0, -1e30)

    loads[0].wait()

    @pl.when(me > 0)
    def _():
        rim_copy((me + n - 1) % n).wait_recv()

    @pl.when(me < n - 1)
    def _():
        rim_copy((me + 1) % n).wait_send()

    def window_cols(col):
        return jnp.concatenate([rim[:, pl.ds(col, 128)], window_kv[:, pl.ds(col, 128)]], 0)

    attend_into(wq, window_cols, rows + WINDOW, bias_w, kx, vx, window_out)

    for load in loads[1:4]:
        load.wait()

    bunches = n // BUNCH

    @pl.loop(0, bunches)
    def _(k):
        base = ((me // BUNCH + k) % bunches) * BUNCH

        @pl.loop(0, BUNCH)
        def _(j):
            @pl.when(base + j != me)
            def _():
                dispatch(base + j, base + j).wait_recv()

        tokens = recv[pl.ds(base, BUNCH)].reshape(BUNCH * cap, width)
        for at, size in tiles(ff):
            gate = jnp.dot(tokens, wg[:, at : at + size], preferred_element_type=jnp.float32)
            up = jnp.dot(tokens, wu[:, at : at + size], preferred_element_type=jnp.float32)
            hid[:, at : at + size] = (gate * jax.nn.sigmoid(gate) * up).astype(jnp.bfloat16)
        for at, size in tiles(width):
            block = jnp.dot(hid[...], wd[:, at : at + size], preferred_element_type=jnp.float32)
            outs[pl.ds(base, BUNCH), :, at : at + size] = block.astype(jnp.bfloat16).reshape(BUNCH, cap, size)

        @pl.loop(0, BUNCH)
        def _(j):
            @pl.when(base + j != me)
            def _():
                give_back(base + j, me).start()

    ret[me] = outs[me]

    @pl.loop(1, n)
    def _(d):
        give_back((me + d) % n, (me + d) % n).wait_recv()

    for at, size in tiles(width):
        total = jnp.zeros((rows, size), jnp.float32)
        returned = ret[:, :, at : at + size].reshape(n * cap, size)
        for i in (2, 1, 0):
            total = total + jnp.dot(combine[i], returned, preferred_element_type=jnp.float32)
        next_out[:, at : at + size] = (stream[:, at : at + size].astype(jnp.float32) + total).astype(jnp.bfloat16)

    for load in loads[4:]:
        load.wait()
    attn_input = normed(next_out[...], attn_gain[...])
    tkv[...] = jnp.dot(attn_input, wp[...], preferred_element_type=jnp.float32).astype(jnp.bfloat16)

    def hand_on(dst, d):
        return pltpu.make_async_remote_copy(
            src_ref=tkv, dst_ref=ctx.at[back - d], send_sem=tract_send.at[d - 1], recv_sem=tract_recv.at[d - 1],
            device_id={"seq": dst}, device_id_type=pl.DeviceIdType.MESH,
        )

    def sends(d):
        return (me + d < n) & (((me + d) * rows + lead) // STRETCH == tract)

    def receives(d):
        return (me - d >= 0) & ((me - d) * rows >= start)

    for d in range(1, back + 1):
        @pl.when(sends(d))
        def _(d=d):
            hand_on((me + d) % n, d).start()

    ctx[back] = tkv[...]
    for d in range(1, back + 1):
        @pl.when(receives(d))
        def _(d=d):
            hand_on((me + n - d) % n, d).wait_recv()

    def tract_cols(col):
        return ctx[:, :, pl.ds(col, 128)].reshape((back + 1) * rows, 128)

    attend_into(tq, tract_cols, (back + 1) * rows, bias_t, kx, vx, tract_out)

    for d in range(1, back + 1):
        @pl.when(sends(d))
        def _(d=d):
            hand_on((me + d) % n, d).wait_send()

    @pl.loop(1, n)
    def _(d):
        dispatch((me + d) % n, me).wait_send()
        give_back((me + d) % n, me).wait_send()


def on_device(
    window_queries, window_kv, stream, moe_gain, routes, route_gates,
    gate_proj, up_proj, down_proj, attn_gain, kv_proj, tract_queries,
):
    n = lax.axis_size("seq")
    rows, width = stream.shape
    split = n // EXPERTS
    cap = rows * TOP // EXPERTS
    ff = gate_proj.shape[1]
    back = STRETCH // rows - 1
    keys = (back + 1) * rows
    vmem = pl.BlockSpec(memory_space=pltpu.VMEM)
    hbm = pl.BlockSpec(memory_space=pl.ANY)
    bf16, f32 = jnp.bfloat16, jnp.float32
    dma = pltpu.SemaphoreType.DMA
    return pl.pallas_call(
        functools.partial(kernel, n, split, back),
        out_shape=(
            jax.ShapeDtypeStruct(window_queries.shape, bf16),
            jax.ShapeDtypeStruct(stream.shape, bf16),
            jax.ShapeDtypeStruct(tract_queries.shape, bf16),
        ),
        in_specs=[vmem] * 6 + [hbm] * 6,
        out_specs=(vmem, vmem, vmem),
        scratch_shapes=[
            pltpu.VMEM(window_queries.shape, bf16),
            pltpu.VMEM(tract_queries.shape, bf16),
            pltpu.VMEM(gate_proj.shape, bf16),
            pltpu.VMEM(up_proj.shape, bf16),
            pltpu.VMEM(down_proj.shape, bf16),
            pltpu.VMEM(kv_proj.shape, bf16),
            pltpu.VMEM((EXPERTS, cap, width), bf16),
            pltpu.VMEM((n, cap, width), bf16),
            pltpu.VMEM((BUNCH * cap, ff), bf16),
            pltpu.VMEM((n, cap, width), bf16),
            pltpu.VMEM((n, cap, width), bf16),
            pltpu.VMEM((3, rows, n * cap), bf16),
            pltpu.VMEM(window_kv.shape, bf16),
            pltpu.VMEM(window_kv.shape, bf16),
            pltpu.VMEM((back + 1,) + window_kv.shape, bf16),
            pltpu.VMEM((rows, rows + WINDOW), f32),
            pltpu.VMEM((rows, keys), f32),
            pltpu.VMEM((2, max(keys, rows + WINDOW), 128), bf16),
            pltpu.VMEM((2, max(keys, rows + WINDOW), 128), bf16),
            dma((6,)), dma((n,)), dma((n,)), dma((n,)), dma((n,)), dma((2,)), dma((max(back, 1),)), dma((max(back, 1),)),
        ],
        compiler_params=pltpu.CompilerParams(
            collective_id=0, has_side_effects=True, vmem_limit_bytes=62 * 2**20
        ),
    )(
        stream, moe_gain[None], routes.T, route_gates.T, attn_gain[None], window_kv,
        window_queries, tract_queries, gate_proj, up_proj, down_proj, kv_proj,
    )


def solution(mesh):
    rows = P(("groups", "seq"), None)
    return jax.shard_map(
        on_device,
        mesh=mesh,
        in_specs=(
            rows, rows, rows, P(), rows, rows,
            P(None, "seq"), P(None, "seq"), P("seq", None), P(), P(), rows,
        ),
        out_specs=(rows, rows, rows),
        check_vma=False,
    )
```

```python
import functools

import jax
import jax.numpy as jnp
from jax import lax
from jax.experimental import pallas as pl
from jax.experimental.pallas import tpu as pltpu
from jax.sharding import PartitionSpec as P

HEADS = 32
KV_HEADS = 4
HEAD_DIM = 64
EXPERTS = 16
TOP = 4
WINDOW = 128
STRETCH = 1024
LOG2E = 1.4426950408889634
TILE = 512
BUNCH = 4


def tiles(width, tile=TILE):
    return [(at, min(tile, width - at)) for at in range(0, width, tile)]


def normed(values, gain):
    widened = values.astype(jnp.float32)
    second = jnp.mean(widened * widened, axis=-1, keepdims=True)
    return (widened * lax.rsqrt(second + 1e-05) * gain).astype(jnp.bfloat16)


def dot_rows(left, right):
    return lax.dot_general(left, right, (((1,), (1,)), ((), ())), preferred_element_type=jnp.float32)


def attend_into(q_ref, read, keys, bias_ref, kx, vx, out_ref):
    half_cols = KV_HEADS * HEAD_DIM
    lane = lax.broadcasted_iota(jnp.int32, (keys, 128), 1) // HEAD_DIM
    pairs = HEADS // KV_HEADS // 2

    @pl.loop(0, KV_HEADS)
    def _(kv):
        side = kv % 2
        for base, ext in ((0, kx), (half_cols, vx)):
            col = pl.multiple_of(base + (kv // 2) * 128, 128)
            both = read(col).astype(jnp.float32)
            same = jnp.where(lane == side, both, 0.0)
            ext[side, 0:keys, :] = same.astype(jnp.bfloat16)
            ext[1 - side, 0:keys, :] = pltpu.roll(same, HEAD_DIM, 1).astype(jnp.bfloat16)

        @pl.loop(0, pairs)
        def _(pair):
            cols = pl.ds(pl.multiple_of((kv * pairs + pair) * 128, 128), 128)
            query = q_ref[:, cols]
            total_out = None
            for parity in range(2):
                scores = lax.dot_general(
                    query, kx[parity, 0:keys, :], (((1,), (1,)), ((), ())),
                    preferred_element_type=jnp.float32,
                ) + bias_ref[...]
                peak = jnp.max(scores, axis=-1, keepdims=True)
                weights = jnp.exp2((scores - peak) * (0.125 * LOG2E))
                totals = jnp.sum(weights, axis=-1, keepdims=True)
                mixed = jnp.dot(
                    weights.astype(jnp.bfloat16), vx[parity, 0:keys, :],
                    preferred_element_type=jnp.float32,
                ) / totals
                total_out = mixed if total_out is None else total_out + mixed
            out_ref[:, cols] = total_out.astype(jnp.bfloat16)


def kernel(
    n, split, back,
    stream, moe_gain, routes_t, gates_t, attn_gain, window_kv,
    window_q_hbm, tract_q_hbm, gate_hbm, up_hbm, down_hbm, proj_hbm,
    window_out, next_out, tract_out,
    wq, tq, wg, wu, wd, wp, send, recv, hid, outs, ret, combine, rim, tkv, ctx, bias_w, bias_t, kx, vx,
    load_sem, send_sem, recv_sem, back_send_sem, back_recv_sem, rim_sem, tract_send, tract_recv,
):
    me = lax.axis_index("seq")
    rows, width = stream.shape
    cap = send.shape[1]
    ff = wg.shape[0]
    loads = [
        pltpu.make_async_copy(src, dst, load_sem.at[i])
        for i, (src, dst) in enumerate(
            ((window_q_hbm, wq), (gate_hbm, wg), (up_hbm, wu), (down_hbm, wd), (proj_hbm, wp), (tract_q_hbm, tq))
        )
    ]

    rim[...] = jnp.zeros_like(rim)
    ctx[...] = jnp.zeros_like(ctx)

    barrier = pltpu.get_barrier_semaphore()

    @pl.loop(1, n)
    def _(d):
        pl.semaphore_signal(barrier, inc=1, device_id={"seq": (me + d) % n}, device_id_type=pl.DeviceIdType.MESH)

    for load in loads:
        load.start()

    expert_id = lax.broadcasted_iota(jnp.int32, (EXPERTS, rows), 0)
    named = jnp.zeros((EXPERTS, rows), jnp.float32)
    gate_of = jnp.zeros((EXPERTS, rows), jnp.float32)
    for k in range(TOP):
        hit = routes_t[k : k + 1, :] == expert_id
        named = named + jnp.where(hit, 1.0, 0.0)
        gate_of = gate_of + jnp.where(hit, gates_t[k : k + 1, :], 0.0)
    earlier = lax.broadcasted_iota(jnp.int32, (rows, rows), 0) < lax.broadcasted_iota(jnp.int32, (rows, rows), 1)
    rank = jnp.dot(
        named.astype(jnp.bfloat16), jnp.where(earlier, 1.0, 0.0).astype(jnp.bfloat16),
        preferred_element_type=jnp.float32,
    )
    rank = jnp.where(named > 0.5, rank, -1.0)
    slot = lax.broadcasted_iota(jnp.int32, (EXPERTS, cap, rows), 1).astype(jnp.float32)
    pick = jnp.where(rank[:, None, :] == slot, 1.0, 0.0)
    moe_input = normed(stream[...], moe_gain[...].reshape(1, width))
    pick_flat = pick.reshape(EXPERTS * cap, rows).astype(jnp.bfloat16)
    for at, size in tiles(width):
        chosen = jnp.dot(pick_flat, moe_input[:, at : at + size], preferred_element_type=jnp.float32)
        send[:, :, at : at + size] = chosen.astype(jnp.bfloat16).reshape(EXPERTS, cap, size)

    pl.semaphore_wait(barrier, n - 1)

    def dispatch(dst, src):
        return pltpu.make_async_remote_copy(
            src_ref=send.at[dst // split], dst_ref=recv.at[src], send_sem=send_sem.at[dst], recv_sem=recv_sem.at[src],
            device_id={"seq": dst}, device_id_type=pl.DeviceIdType.MESH,
        )

    def give_back(dst, src):
        return pltpu.make_async_remote_copy(
            src_ref=outs.at[dst], dst_ref=ret.at[src], send_sem=back_send_sem.at[dst], recv_sem=back_recv_sem.at[src],
            device_id={"seq": dst}, device_id_type=pl.DeviceIdType.MESH,
        )

    def rim_copy(dst):
        return pltpu.make_async_remote_copy(
            src_ref=window_kv, dst_ref=rim, send_sem=rim_sem.at[0], recv_sem=rim_sem.at[1],
            device_id={"seq": dst}, device_id_type=pl.DeviceIdType.MESH,
        )

    @pl.when(me < n - 1)
    def _():
        rim_copy((me + 1) % n).start()

    @pl.loop(1, n)
    def _(d):
        dispatch((me + d) % n, me).start()

    recv[me] = send[me // split]

    gated = (pick * gate_of[:, None, :])[:, None]
    gated = jnp.broadcast_to(gated, (EXPERTS, split, cap, rows)).reshape(n * cap, rows)
    rest = gated.T
    for i in range(3):
        term = rest.astype(jnp.bfloat16)
        combine[i] = term
        rest = rest - term.astype(jnp.float32)

    row_w = lax.broadcasted_iota(jnp.int32, (rows, rows + WINDOW), 0)
    col_w = lax.broadcasted_iota(jnp.int32, (rows, rows + WINDOW), 1)
    distance = row_w - (col_w - WINDOW)
    seen = (distance >= 0) & (distance < WINDOW) & (me * rows + col_w - WINDOW >= 0)
    bias_w[...] = jnp.where(seen, 0.0, -1e30)
    first = me * rows
    row_t = lax.broadcasted_iota(jnp.int32, bias_t.shape, 0) + first
    col_t = lax.broadcasted_iota(jnp.int32, bias_t.shape, 1) + (first - back * rows)
    lead = STRETCH // 2
    tract = (first + lead) // STRETCH
    start = tract * STRETCH - lead
    seen = (col_t <= row_t) & (col_t >= 0) & (col_t >= start)
    bias_t[...] = jnp.where(seen, 0.0, -1e30)

    loads[0].wait()

    @pl.when(me > 0)
    def _():
        rim_copy((me + n - 1) % n).wait_recv()

    @pl.when(me < n - 1)
    def _():
        rim_copy((me + 1) % n).wait_send()

    def window_cols(col):
        return jnp.concatenate([rim[:, pl.ds(col, 128)], window_kv[:, pl.ds(col, 128)]], 0)

    attend_into(wq, window_cols, rows + WINDOW, bias_w, kx, vx, window_out)

    for load in loads[1:4]:
        load.wait()

    bunches = n // BUNCH

    @pl.loop(0, bunches)
    def _(k):
        base = ((me // BUNCH + k) % bunches) * BUNCH

        @pl.loop(0, BUNCH)
        def _(j):
            @pl.when(base + j != me)
            def _():
                dispatch(base + j, base + j).wait_recv()

        tokens = recv[pl.ds(base, BUNCH)].reshape(BUNCH * cap, width)
        for at, size in tiles(ff):
            gate = dot_rows(tokens, wg[at : at + size, :])
            up = dot_rows(tokens, wu[at : at + size, :])
            hid[:, at : at + size] = (gate * jax.nn.sigmoid(gate) * up).astype(jnp.bfloat16)
        for at, size in tiles(width):
            block = jnp.dot(hid[...], wd[:, at : at + size], preferred_element_type=jnp.float32)
            outs[pl.ds(base, BUNCH), :, at : at + size] = block.astype(jnp.bfloat16).reshape(BUNCH, cap, size)

        @pl.loop(0, BUNCH)
        def _(j):
            @pl.when(base + j != me)
            def _():
                give_back(base + j, me).start()

    ret[me] = outs[me]

    @pl.loop(1, n)
    def _(d):
        give_back((me + d) % n, (me + d) % n).wait_recv()

    for at, size in tiles(width):
        total = jnp.zeros((rows, size), jnp.float32)
        returned = ret[:, :, at : at + size].reshape(n * cap, size)
        for i in (2, 1, 0):
            total = total + jnp.dot(combine[i], returned, preferred_element_type=jnp.float32)
        next_out[:, at : at + size] = (stream[:, at : at + size].astype(jnp.float32) + total).astype(jnp.bfloat16)

    for load in loads[4:]:
        load.wait()
    attn_input = normed(next_out[...], attn_gain[...].reshape(1, width))
    tkv[...] = jnp.dot(attn_input, wp[...], preferred_element_type=jnp.float32).astype(jnp.bfloat16)

    def hand_on(dst, d):
        return pltpu.make_async_remote_copy(
            src_ref=tkv, dst_ref=ctx.at[back - d], send_sem=tract_send.at[d - 1], recv_sem=tract_recv.at[d - 1],
            device_id={"seq": dst}, device_id_type=pl.DeviceIdType.MESH,
        )

    def sends(d):
        return (me + d < n) & (((me + d) * rows + lead) // STRETCH == tract)

    def receives(d):
        return (me - d >= 0) & ((me - d) * rows >= start)

    for d in range(1, back + 1):
        @pl.when(sends(d))
        def _(d=d):
            hand_on((me + d) % n, d).start()

    ctx[back] = tkv[...]
    for d in range(1, back + 1):
        @pl.when(receives(d))
        def _(d=d):
            hand_on((me + n - d) % n, d).wait_recv()

    def tract_cols(col):
        return ctx[:, :, pl.ds(col, 128)].reshape((back + 1) * rows, 128)

    attend_into(tq, tract_cols, (back + 1) * rows, bias_t, kx, vx, tract_out)

    for d in range(1, back + 1):
        @pl.when(sends(d))
        def _(d=d):
            hand_on((me + d) % n, d).wait_send()

    @pl.loop(1, n)
    def _(d):
        dispatch((me + d) % n, me).wait_send()
        give_back((me + d) % n, me).wait_send()


def on_device(
    window_queries, window_kv, stream, moe_gain, routes, route_gates,
    gate_proj, up_proj, down_proj, attn_gain, kv_proj, tract_queries,
):
    n = lax.axis_size("seq")
    rows, width = stream.shape
    split = n // EXPERTS
    cap = rows * TOP // EXPERTS
    ff = gate_proj.shape[1]
    back = STRETCH // rows - 1
    keys = (back + 1) * rows
    vmem = pl.BlockSpec(memory_space=pltpu.VMEM)
    hbm = pl.BlockSpec(memory_space=pl.ANY)
    bf16, f32 = jnp.bfloat16, jnp.float32
    dma = pltpu.SemaphoreType.DMA
    return pl.pallas_call(
        functools.partial(kernel, n, split, back),
        out_shape=(
            jax.ShapeDtypeStruct(window_queries.shape, bf16),
            jax.ShapeDtypeStruct(stream.shape, bf16),
            jax.ShapeDtypeStruct(tract_queries.shape, bf16),
        ),
        in_specs=[vmem] * 6 + [hbm] * 6,
        out_specs=(vmem, vmem, vmem),
        scratch_shapes=[
            pltpu.VMEM(window_queries.shape, bf16),
            pltpu.VMEM(tract_queries.shape, bf16),
            pltpu.VMEM((ff, width), bf16),
            pltpu.VMEM((ff, width), bf16),
            pltpu.VMEM(down_proj.shape, bf16),
            pltpu.VMEM(kv_proj.shape, bf16),
            pltpu.VMEM((EXPERTS, cap, width), bf16),
            pltpu.VMEM((n, cap, width), bf16),
            pltpu.VMEM((BUNCH * cap, ff), bf16),
            pltpu.VMEM((n, cap, width), bf16),
            pltpu.VMEM((n, cap, width), bf16),
            pltpu.VMEM((3, rows, n * cap), bf16),
            pltpu.VMEM(window_kv.shape, bf16),
            pltpu.VMEM(window_kv.shape, bf16),
            pltpu.VMEM((back + 1,) + window_kv.shape, bf16),
            pltpu.VMEM((rows, rows + WINDOW), f32),
            pltpu.VMEM((rows, keys), f32),
            pltpu.VMEM((2, max(keys, rows + WINDOW), 128), bf16),
            pltpu.VMEM((2, max(keys, rows + WINDOW), 128), bf16),
            dma((6,)), dma((n,)), dma((n,)), dma((n,)), dma((n,)), dma((2,)), dma((max(back, 1),)), dma((max(back, 1),)),
        ],
        compiler_params=pltpu.CompilerParams(
            collective_id=0, has_side_effects=True, vmem_limit_bytes=62 * 2**20
        ),
    )(
        stream, moe_gain, routes.T, route_gates.T, attn_gain, window_kv,
        window_queries, tract_queries, gate_proj.T, up_proj.T, down_proj, kv_proj,
    )


def solution(mesh):
    rows = P(("groups", "seq"), None)
    return jax.shard_map(
        on_device,
        mesh=mesh,
        in_specs=(
            rows, rows, rows, P(), rows, rows,
            P(None, "seq"), P(None, "seq"), P("seq", None), P(), P(), rows,
        ),
        out_specs=(rows, rows, rows),
        check_vma=False,
    )
```

```python
import functools

import jax
import jax.numpy as jnp
from jax import lax
from jax.experimental import pallas as pl
from jax.experimental.pallas import tpu as pltpu
from jax.sharding import PartitionSpec as P

HEADS = 32
KV_HEADS = 4
HEAD_DIM = 64
EXPERTS = 16
TOP = 4
WINDOW = 128
STRETCH = 1024
LOG2E = 1.4426950408889634
TILE = 512
BUNCH = 4


def tiles(width, tile=TILE):
    return [(at, min(tile, width - at)) for at in range(0, width, tile)]


def normed(values, gain):
    widened = values.astype(jnp.float32)
    second = jnp.mean(widened * widened, axis=-1, keepdims=True)
    return (widened * lax.rsqrt(second + 1e-05) * gain).astype(jnp.bfloat16)


def dot_rows(left, right):
    return lax.dot_general(left, right, (((1,), (1,)), ((), ())), preferred_element_type=jnp.float32)


def attend_into(q_ref, read, keys, bias_ref, kx, vx, out_ref):
    half_cols = KV_HEADS * HEAD_DIM
    lane = lax.broadcasted_iota(jnp.int32, (keys, 128), 1) // HEAD_DIM
    pairs = HEADS // KV_HEADS // 2

    @pl.loop(0, KV_HEADS)
    def _(kv):
        side = kv % 2
        for base, ext in ((0, kx), (half_cols, vx)):
            col = pl.multiple_of(base + (kv // 2) * 128, 128)
            both = read(col).astype(jnp.float32)
            same = jnp.where(lane == side, both, 0.0)
            ext[side, 0:keys, :] = same.astype(jnp.bfloat16)
            ext[1 - side, 0:keys, :] = pltpu.roll(same, HEAD_DIM, 1).astype(jnp.bfloat16)

        @pl.loop(0, pairs)
        def _(pair):
            cols = pl.ds(pl.multiple_of((kv * pairs + pair) * 128, 128), 128)
            query = q_ref[:, cols]
            total_out = None
            for parity in range(2):
                scores = lax.dot_general(
                    query, kx[parity, 0:keys, :], (((1,), (1,)), ((), ())),
                    preferred_element_type=jnp.float32,
                ) + bias_ref[...]
                peak = jnp.max(scores, axis=-1, keepdims=True)
                weights = jnp.exp2((scores - peak) * (0.125 * LOG2E))
                totals = jnp.sum(weights, axis=-1, keepdims=True)
                mixed = jnp.dot(
                    weights.astype(jnp.bfloat16), vx[parity, 0:keys, :],
                    preferred_element_type=jnp.float32,
                ) / totals
                total_out = mixed if total_out is None else total_out + mixed
            out_ref[:, cols] = total_out.astype(jnp.bfloat16)


def kernel(
    n, split, back,
    stream, moe_gain, info, attn_gain, window_kv,
    window_q_hbm, tract_q_hbm, gate_hbm, up_hbm, down_hbm, proj_hbm,
    window_out, next_out, tract_out,
    wq, tq, wg, wu, wd, wp, send, recv, hid, outs, ret, combine, mine, theirs, info_p, part, part_in, rim, tkv, ctx, bias_w, bias_t, kx, vx,
    load_sem, send_sem, recv_sem, back_send_sem, back_recv_sem, rim_sem, pair_sem, tract_send, tract_recv,
):
    me = lax.axis_index("seq")
    rows, width = stream.shape
    cap = send.shape[2]
    half = n // 2
    experts = EXPERTS // 2
    here = (me // half) * half
    mate = (me + half) % n
    place = me - here
    ff = wg.shape[0]
    loads = [
        pltpu.make_async_copy(src, dst, load_sem.at[i])
        for i, (src, dst) in enumerate(
            ((window_q_hbm, wq), (gate_hbm, wg), (up_hbm, wu), (down_hbm, wd), (proj_hbm, wp), (tract_q_hbm, tq))
        )
    ]

    rim[...] = jnp.zeros_like(rim)
    ctx[...] = jnp.zeros_like(ctx)

    barrier = pltpu.get_barrier_semaphore()

    @pl.loop(1, n)
    def _(d):
        pl.semaphore_signal(barrier, inc=1, device_id={"seq": (me + d) % n}, device_id_type=pl.DeviceIdType.MESH)

    for load in loads:
        load.start()

    mine[...] = normed(stream[...], moe_gain[...].reshape(1, width))

    pl.semaphore_wait(barrier, n - 1)

    def pair_copy(i, src, dst):
        return pltpu.make_async_remote_copy(
            src_ref=src, dst_ref=dst, send_sem=pair_sem.at[0, i], recv_sem=pair_sem.at[1, i],
            device_id={"seq": mate}, device_id_type=pl.DeviceIdType.MESH,
        )

    info_copy = pair_copy(0, info, info_p)
    block_copy = pair_copy(1, mine, theirs)
    part_copy = pair_copy(2, part, part_in)
    block_copy.start()
    info_copy.start()

    def dispatch(who, dst, src):
        return pltpu.make_async_remote_copy(
            src_ref=send.at[who, (here + dst) // split - here // split], dst_ref=recv.at[who, src],
            send_sem=send_sem.at[who, dst], recv_sem=recv_sem.at[who, src],
            device_id={"seq": here + dst}, device_id_type=pl.DeviceIdType.MESH,
        )

    def give_back(who, dst, src):
        return pltpu.make_async_remote_copy(
            src_ref=outs.at[who, dst], dst_ref=ret.at[who, src],
            send_sem=back_send_sem.at[who, dst], recv_sem=back_recv_sem.at[who, src],
            device_id={"seq": here + dst}, device_id_type=pl.DeviceIdType.MESH,
        )

    def spread(who, info_ref, block_ref):
        first_expert = here // split
        expert_id = (lax.broadcasted_iota(jnp.int32, (experts, rows), 0) + first_expert).astype(jnp.float32)
        named = jnp.zeros((experts, rows), jnp.float32)
        gate_of = jnp.zeros((experts, rows), jnp.float32)
        for k in range(TOP):
            hit = info_ref[k : k + 1, :] == expert_id
            named = named + jnp.where(hit, 1.0, 0.0)
            gate_of = gate_of + jnp.where(hit, info_ref[TOP + k : TOP + k + 1, :], 0.0)
        earlier = lax.broadcasted_iota(jnp.int32, (rows, rows), 0) < lax.broadcasted_iota(jnp.int32, (rows, rows), 1)
        rank = jnp.dot(
            named.astype(jnp.bfloat16), jnp.where(earlier, 1.0, 0.0).astype(jnp.bfloat16),
            preferred_element_type=jnp.float32,
        )
        rank = jnp.where(named > 0.5, rank, -1.0)
        slot = lax.broadcasted_iota(jnp.int32, (experts, cap, rows), 1).astype(jnp.float32)
        pick = jnp.where(rank[:, None, :] == slot, 1.0, 0.0)
        pick_flat = pick.reshape(experts * cap, rows).astype(jnp.bfloat16)
        for at, size in tiles(width):
            chosen = jnp.dot(pick_flat, block_ref[:, at : at + size], preferred_element_type=jnp.float32)
            send[who, :, :, at : at + size] = chosen.astype(jnp.bfloat16).reshape(experts, cap, size)

        @pl.loop(1, half)
        def _(d):
            dispatch(who, (place + d) % half, place).start()

        recv[who, place] = send[who, me // split - here // split]
        gated = (pick * gate_of[:, None, :])[:, None]
        gated = jnp.broadcast_to(gated, (experts, split, cap, rows)).reshape(half * cap, rows)
        rest = gated.T
        for i in range(3):
            term = rest.astype(jnp.bfloat16)
            combine[who, i] = term
            rest = rest - term.astype(jnp.float32)

    def run(who):
        bunches = half // BUNCH

        @pl.loop(0, bunches)
        def _(k):
            base = ((place // BUNCH + k) % bunches) * BUNCH

            @pl.loop(0, BUNCH)
            def _(j):
                @pl.when(base + j != place)
                def _():
                    dispatch(who, base + j, base + j).wait_recv()

            tokens = recv[who, pl.ds(base, BUNCH)].reshape(BUNCH * cap, width)
            for at, size in tiles(ff):
                gate = dot_rows(tokens, wg[at : at + size, :])
                up = dot_rows(tokens, wu[at : at + size, :])
                hid[:, at : at + size] = (gate * jax.nn.sigmoid(gate) * up).astype(jnp.bfloat16)
            for at, size in tiles(width):
                block = jnp.dot(hid[...], wd[:, at : at + size], preferred_element_type=jnp.float32)
                outs[who, pl.ds(base, BUNCH), :, at : at + size] = block.astype(jnp.bfloat16).reshape(BUNCH, cap, size)

            @pl.loop(0, BUNCH)
            def _(j):
                @pl.when(base + j != place)
                def _():
                    give_back(who, base + j, place).start()

        ret[who, place] = outs[who, place]

    def gathered(who, at, size):
        total = jnp.zeros((rows, size), jnp.float32)
        returned = ret[who, :, :, at : at + size].reshape(half * cap, size)
        for i in (2, 1, 0):
            total = total + jnp.dot(combine[who, i], returned, preferred_element_type=jnp.float32)
        return total

    def all_back(who):
        @pl.loop(1, half)
        def _(d):
            give_back(who, (place + d) % half, (place + d) % half).wait_recv()

    def rim_copy(dst):
        return pltpu.make_async_remote_copy(
            src_ref=window_kv, dst_ref=rim, send_sem=rim_sem.at[0], recv_sem=rim_sem.at[1],
            device_id={"seq": dst}, device_id_type=pl.DeviceIdType.MESH,
        )

    @pl.when(me < n - 1)
    def _():
        rim_copy((me + 1) % n).start()

    spread(0, info, mine)

    row_w = lax.broadcasted_iota(jnp.int32, (rows, rows + WINDOW), 0)
    col_w = lax.broadcasted_iota(jnp.int32, (rows, rows + WINDOW), 1)
    distance = row_w - (col_w - WINDOW)
    seen = (distance >= 0) & (distance < WINDOW) & (me * rows + col_w - WINDOW >= 0)
    bias_w[...] = jnp.where(seen, 0.0, -1e30)
    first = me * rows
    row_t = lax.broadcasted_iota(jnp.int32, bias_t.shape, 0) + first
    col_t = lax.broadcasted_iota(jnp.int32, bias_t.shape, 1) + (first - back * rows)
    lead = STRETCH // 2
    tract = (first + lead) // STRETCH
    start = tract * STRETCH - lead
    seen = (col_t <= row_t) & (col_t >= 0) & (col_t >= start)
    bias_t[...] = jnp.where(seen, 0.0, -1e30)

    loads[0].wait()

    @pl.when(me > 0)
    def _():
        rim_copy((me + n - 1) % n).wait_recv()

    @pl.when(me < n - 1)
    def _():
        rim_copy((me + 1) % n).wait_send()

    def window_cols(col):
        return jnp.concatenate([rim[:, pl.ds(col, 128)], window_kv[:, pl.ds(col, 128)]], 0)

    attend_into(wq, window_cols, rows + WINDOW, bias_w, kx, vx, window_out)

    for load in loads[1:4]:
        load.wait()

    info_copy.wait()
    block_copy.wait()
    spread(1, info_p, theirs)
    run(0)
    run(1)
    all_back(1)
    for at, size in tiles(width):
        part[:, at : at + size] = gathered(1, at, size).astype(jnp.bfloat16)
    part_copy.start()
    all_back(0)
    part_copy.wait_recv()
    for at, size in tiles(width):
        total = gathered(0, at, size) + part_in[:, at : at + size].astype(jnp.float32)
        next_out[:, at : at + size] = (stream[:, at : at + size].astype(jnp.float32) + total).astype(jnp.bfloat16)

    for load in loads[4:]:
        load.wait()
    attn_input = normed(next_out[...], attn_gain[...].reshape(1, width))
    tkv[...] = jnp.dot(attn_input, wp[...], preferred_element_type=jnp.float32).astype(jnp.bfloat16)

    def hand_on(dst, d):
        return pltpu.make_async_remote_copy(
            src_ref=tkv, dst_ref=ctx.at[back - d], send_sem=tract_send.at[d - 1], recv_sem=tract_recv.at[d - 1],
            device_id={"seq": dst}, device_id_type=pl.DeviceIdType.MESH,
        )

    def sends(d):
        return (me + d < n) & (((me + d) * rows + lead) // STRETCH == tract)

    def receives(d):
        return (me - d >= 0) & ((me - d) * rows >= start)

    for d in range(1, back + 1):
        @pl.when(sends(d))
        def _(d=d):
            hand_on((me + d) % n, d).start()

    ctx[back] = tkv[...]
    for d in range(1, back + 1):
        @pl.when(receives(d))
        def _(d=d):
            hand_on((me + n - d) % n, d).wait_recv()

    def tract_cols(col):
        return ctx[:, :, pl.ds(col, 128)].reshape((back + 1) * rows, 128)

    attend_into(tq, tract_cols, (back + 1) * rows, bias_t, kx, vx, tract_out)

    for d in range(1, back + 1):
        @pl.when(sends(d))
        def _(d=d):
            hand_on((me + d) % n, d).wait_send()

    part_copy.wait_send()
    for who in range(2):
        @pl.loop(1, half)
        def _(d, who=who):
            dispatch(who, (place + d) % half, place).wait_send()
            give_back(who, (place + d) % half, place).wait_send()


def on_device(
    window_queries, window_kv, stream, moe_gain, routes, route_gates,
    gate_proj, up_proj, down_proj, attn_gain, kv_proj, tract_queries,
):
    n = lax.axis_size("seq")
    rows, width = stream.shape
    split = n // EXPERTS
    cap = rows * TOP // EXPERTS
    ff = gate_proj.shape[1]
    back = STRETCH // rows - 1
    keys = (back + 1) * rows
    vmem = pl.BlockSpec(memory_space=pltpu.VMEM)
    hbm = pl.BlockSpec(memory_space=pl.ANY)
    bf16, f32 = jnp.bfloat16, jnp.float32
    dma = pltpu.SemaphoreType.DMA
    return pl.pallas_call(
        functools.partial(kernel, n, split, back),
        out_shape=(
            jax.ShapeDtypeStruct(window_queries.shape, bf16),
            jax.ShapeDtypeStruct(stream.shape, bf16),
            jax.ShapeDtypeStruct(tract_queries.shape, bf16),
        ),
        in_specs=[vmem] * 5 + [hbm] * 6,
        out_specs=(vmem, vmem, vmem),
        scratch_shapes=[
            pltpu.VMEM(window_queries.shape, bf16),
            pltpu.VMEM(tract_queries.shape, bf16),
            pltpu.VMEM((ff, width), bf16),
            pltpu.VMEM((ff, width), bf16),
            pltpu.VMEM(down_proj.shape, bf16),
            pltpu.VMEM(kv_proj.shape, bf16),
            pltpu.VMEM((2, EXPERTS // 2, cap, width), bf16),
            pltpu.VMEM((2, n // 2, cap, width), bf16),
            pltpu.VMEM((BUNCH * cap, ff), bf16),
            pltpu.VMEM((2, n // 2, cap, width), bf16),
            pltpu.VMEM((2, n // 2, cap, width), bf16),
            pltpu.VMEM((2, 3, rows, n // 2 * cap), bf16),
            pltpu.VMEM((rows, width), bf16),
            pltpu.VMEM((rows, width), bf16),
            pltpu.VMEM((2 * TOP, rows), f32),
            pltpu.VMEM((rows, width), bf16),
            pltpu.VMEM((rows, width), bf16),
            pltpu.VMEM(window_kv.shape, bf16),
            pltpu.VMEM(window_kv.shape, bf16),
            pltpu.VMEM((back + 1,) + window_kv.shape, bf16),
            pltpu.VMEM((rows, rows + WINDOW), f32),
            pltpu.VMEM((rows, keys), f32),
            pltpu.VMEM((2, max(keys, rows + WINDOW), 128), bf16),
            pltpu.VMEM((2, max(keys, rows + WINDOW), 128), bf16),
            dma((6,)), dma((2, n // 2)), dma((2, n // 2)), dma((2, n // 2)), dma((2, n // 2)), dma((2,)), dma((2, 3)), dma((max(back, 1),)), dma((max(back, 1),)),
        ],
        compiler_params=pltpu.CompilerParams(
            collective_id=0, has_side_effects=True, vmem_limit_bytes=62 * 2**20
        ),
    )(
        stream, moe_gain, jnp.concatenate([routes.T.astype(f32), route_gates.T], 0), attn_gain, window_kv,
        window_queries, tract_queries, gate_proj.T, up_proj.T, down_proj, kv_proj,
    )


def solution(mesh):
    rows = P(("groups", "seq"), None)
    return jax.shard_map(
        on_device,
        mesh=mesh,
        in_specs=(
            rows, rows, rows, P(), rows, rows,
            P(None, "seq"), P(None, "seq"), P("seq", None), P(), P(), rows,
        ),
        out_specs=(rows, rows, rows),
        check_vma=False,
    )
```
